32 devices in a mesh: pair: 16 (over z, x, core), slab: 2 (over y).
Axes of the slice: x: 2, y: 2, z: 4, core: 2. Of those that a mesh axis runs over, the one named last changes fastest.
Arguments:
- amps: bfloat16 [64, 256, 128], P(('pair', 'slab')), may hold values from -6 to 6
- symmetry: int32 [256], replicated, may hold values from 0 to 3
- screen: int32 [16, 16, 16], P('pair'), may hold values 0 or 1
- owner: int32 [256], replicated, may hold values from 0 to 15, as said below
- integrals: bfloat16 [16, 2048, 2048], P('pair', 'slab'), may hold values from -0.25 to 0.25
Outputs:
- residual: bfloat16 [64, 16, 16, 128], P(('pair', 'slab'))
The draws below stay inside these ranges and needn't reach their ends.
Inputs may be any that keep to these rules, and one draw needn't show every extreme that they name: Every owner from 0 to 15 holds exactly 16 tiles.
All inputs are finite; a program needn't handle non-finite values. No bound on the sum of `screen` on one device may be relied on, other than what follows from the above.
Results may differ from the reference program's by a relative error of at most 0.001.
Values may be sent and summed in bfloat16 or wider, within the bound.
No kernel may reach another device: no remote copies, remote signals or barrier semaphores. Data moves between devices by JAX's collectives and lax.ppermute only.
A program may use at most 64 MiB of HBM per device.

```python
import math
import jax
import jax.numpy as jnp
import numpy as np
from jax import lax

PT = 128
TILE_DEV = 16
NSYM = 4
NT = 256
KD = 2048
OCCP = 64
N_PAIR = 16


def draw_owner(key, part):
    return (jax.random.permutation(key, NT) // TILE_DEV).astype(jnp.int32)


def touch_ends(entries, rng, least, largest):
    index_at = [jax.random.randint(jax.random.fold_in(rng, axis), (), 0, length) for axis, length in enumerate(entries.shape)]
    longest = entries.shape.index(max(entries.shape))
    beside = index_at[:longest] + [(index_at[longest] + 1) % entries.shape[longest]] + index_at[longest + 1:]
    return entries.at[tuple(index_at)].set(least).at[tuple(beside)].set(largest)


def level_of(stream_key, extent, cuts, low, largest):
    factor_of = 1.0
    for dim, shards_of in cuts:
        steps = jax.random.uniform(jax.random.fold_in(jax.random.fold_in(stream_key, 6), dim), (shards_of,), jnp.float32, low / len(cuts), largest / len(cuts))
        factor_of = factor_of * jnp.repeat(jnp.exp(steps), extent[dim] // shards_of).reshape((-1,) + (1,) * (len(extent) - 1 - dim))
    return factor_of


def cumulative_ranks(count, lean):
    portions = [(1 << 20) // math.isqrt(standing ** lean) + 1 for standing in range(1, count + 1)]
    spread = 1 + sum(portions) // (1 << 30)
    return np.cumsum(np.array([max(1, weight // spread) for weight in portions]))


def skewed_ids(rng, extent, count, lean):
    grid = cumulative_ranks(count, lean)
    ticket = jax.random.randint(jax.random.fold_in(rng, 1), extent, 0, int(grid[count - 1]))
    grade = jnp.searchsorted(jnp.asarray(grid, jnp.int32), ticket, side="right")
    return jax.random.permutation(jax.random.fold_in(rng, 2), count)[grade].astype(jnp.int32)


def scatter_about(rng, shape, spread, reach, shards=(), kind=jnp.bfloat16):
    factor_of = level_of(rng, shape, shards, -0.22, 0.18) if shards else 1.0
    drawn = jax.random.normal(rng, shape, jnp.float32) * spread * factor_of
    return jnp.minimum(jnp.maximum(drawn, -reach), reach).astype(kind)


def setup_inputs(seed: int = 0) -> dict:
    keys = jax.random.split(jax.random.key(seed), 6)
    return {
        "amps": scatter_about(keys[0], (OCCP, NT, PT), 1.0, 6.0, ((0, 32),)),
        "symmetry": touch_ends(skewed_ids(keys[1], (NT,), NSYM, 2), jax.random.fold_in(keys[1], 3), 0, NSYM - 1).astype(jnp.int32),
        "screen": touch_ends((jax.random.randint(keys[2], (N_PAIR, TILE_DEV, TILE_DEV), 0, 4) < 3).astype(jnp.int32), jax.random.fold_in(keys[2], 1), 0, 1),
        "owner": draw_owner(jax.random.fold_in(keys[5], 71), 0),
        "integrals": scatter_about(keys[4], (N_PAIR, KD, KD), (KD // 4) ** -0.5, 0.25, ((0, 16), (1, 2))),
    }


def reference(amps, symmetry, screen, owner, integrals):
    tile_order = jnp.argsort(owner, stable=True).astype(jnp.int32).reshape(N_PAIR, TILE_DEV)
    labels = jnp.take(symmetry, tile_order)
    allowed = ((labels[:, :, None] == labels[:, None, :]) & (screen == 1)).astype(jnp.bfloat16)

    def one_owner(owner_index):
        owned = lax.dynamic_index_in_dim(tile_order, owner_index, 0, keepdims=False)
        gathered = jnp.take(amps, owned, axis=1).reshape(OCCP, KD)
        mask_rows = jnp.repeat(lax.dynamic_index_in_dim(allowed, owner_index, 0, keepdims=False), PT, axis=0)
        block_rows = lax.dynamic_index_in_dim(integrals, owner_index, 0, keepdims=False)
        masked = (block_rows.reshape(KD, TILE_DEV, PT) * mask_rows[:, :, None]).reshape(KD, KD)
        return jnp.dot(gathered, masked, preferred_element_type=jnp.float32).astype(jnp.bfloat16)

    blocks = lax.map(one_owner, jnp.arange(N_PAIR, dtype=jnp.int32))
    return jnp.transpose(blocks, (1, 0, 2)).reshape(OCCP, N_PAIR, TILE_DEV, PT)
```

```python
import functools

import jax
import jax.numpy as jnp
from jax import lax
from jax.experimental import pallas as pl
from jax.experimental.pallas import tpu as pltpu
from jax.sharding import PartitionSpec as P

LANES = 128
CODE_MAX = 32767.0
SCALE_STEPS = 128.0
LEAST = 1e-37
VMEM_LIMIT = 48 * 1024 * 1024


def tile_places(owner_ref, owners, per_owner):
    pieces = owner_ref.shape[0]
    tiles = pieces * LANES
    rows = lax.broadcasted_iota(jnp.int32, (owners, LANES), 0)
    held = jnp.concatenate(
        [(owner_ref[j : j + 1, :] == rows).astype(jnp.float32) for j in range(pieces)], axis=1
    )
    earlier = (
        lax.broadcasted_iota(jnp.int32, (tiles, tiles), 0)
        < lax.broadcasted_iota(jnp.int32, (tiles, tiles), 1)
    ).astype(jnp.bfloat16)
    rank = jnp.dot(held.astype(jnp.bfloat16), earlier, preferred_element_type=jnp.float32)
    first = lax.broadcasted_iota(jnp.int32, (owners, tiles), 0).astype(jnp.float32) * per_owner
    return jnp.sum(held * (first + rank), axis=0, keepdims=True)


def order_kernel(owners, owner_ref, amps_ref, out_ref):
    local_rows, tiles, width = amps_ref.shape
    place = tile_places(owner_ref, owners, tiles // owners)
    rows = lax.broadcasted_iota(jnp.int32, (tiles, tiles), 0).astype(jnp.float32)
    pick = (rows == place).astype(jnp.bfloat16)
    for i in range(local_rows):
        out_ref[:, i * width : (i + 1) * width] = jnp.dot(
            pick, amps_ref[i], preferred_element_type=jnp.float32
        ).astype(out_ref.dtype)


def mask_kernel(owners, owner_ref, symmetry_ref, screen_ref, block_ref, out_ref, wide):
    step = pl.program_id(0)
    per_owner = screen_ref.shape[1]
    width, columns = block_ref.shape

    @pl.when(step == 0)
    def _():
        pieces = owner_ref.shape[0]
        tiles = pieces * LANES
        place = tile_places(owner_ref, owners, per_owner)
        first = lax.axis_index("pair") * per_owner
        rows = (lax.broadcasted_iota(jnp.int32, (per_owner, tiles), 0) + first).astype(jnp.float32)
        mine = (rows == place).astype(jnp.bfloat16)
        classes = lax.broadcasted_iota(jnp.int32, (16, LANES), 0)
        kinds = jnp.concatenate(
            [
                (symmetry_ref[j : j + 1, :] == classes).astype(jnp.float32)
                for j in range(pieces)
            ],
            axis=1,
        ).astype(jnp.bfloat16)
        across = (((1,), (1,)), ((), ()))
        labels = lax.dot_general(mine, kinds, across, preferred_element_type=jnp.float32)
        labels = labels.astype(jnp.bfloat16)
        same = lax.dot_general(labels, labels, across, preferred_element_type=jnp.float32)
        allowed = jnp.where(screen_ref[0] == 1, same, 0.0).astype(jnp.bfloat16)
        spread = (
            lax.broadcasted_iota(jnp.int32, (per_owner, columns), 1) // width
            == lax.broadcasted_iota(jnp.int32, (per_owner, columns), 0)
        ).astype(jnp.bfloat16)
        wide[...] = jnp.dot(allowed, spread, preferred_element_type=jnp.float32)

    here = lax.axis_index("slab") * pl.num_programs(0) + step
    keep = wide[pl.ds(here, 1), :].astype(block_ref.dtype)
    start = pl.multiple_of(step * width, width)
    out_ref[pl.ds(start, width), :] = block_ref[...] * keep


def partial_kernel(devices, local_rows, amps_ref, block_ref, out_ref, flat, operand):
    width = LANES
    tiles_here = block_ref.shape[0] // width
    per_owner = block_ref.shape[1] // width
    pitch = per_owner + 1
    for i in range(local_rows):
        flat[i] = amps_ref[:, i * width : (i + 1) * width].astype(jnp.float32)
        for k in range(tiles_here):
            operand[i * devices : (i + 1) * devices, k * width : (k + 1) * width] = flat[
                i, pl.ds(k, devices, stride=tiles_here), :
            ].astype(operand.dtype)
    lane = lax.broadcasted_iota(jnp.int32, (devices, width), 1)
    scales = jnp.zeros((devices, width), jnp.int32)
    for pair in range(per_owner // 2):
        summed = jnp.dot(
            operand[...],
            block_ref[:, pair * 2 * width : (pair + 1) * 2 * width],
            preferred_element_type=jnp.float32,
        )
        for half in range(2):
            tile = pair * 2 + half
            words = []
            for i in range(2):
                value = summed[i * devices : (i + 1) * devices, half * width : (half + 1) * width]
                top = jnp.maximum(jnp.max(jnp.abs(value), axis=1, keepdims=True), LEAST)
                code = jnp.ceil(jnp.log2(top) * SCALE_STEPS) + 1.0
                grain = jnp.exp2(code * (-1.0 / SCALE_STEPS)) * CODE_MAX
                words.append(
                    (jnp.floor(value * grain + 0.5).astype(jnp.int32), code.astype(jnp.int32))
                )
            (low, low_code), (high, high_code) = words
            out_ref[pl.ds(tile, devices, stride=pitch), :] = (high << 16) | (low & 0xFFFF)
            scales = jnp.where(lane == tile, (high_code << 16) | (low_code & 0xFFFF), scales)
    out_ref[pl.ds(per_owner, devices, stride=pitch), :] = scales


def total_kernel(slabs, coded_ref, out_ref):
    local_rows, owners, per_owner, width = out_ref.shape
    devices = owners * slabs
    pitch = per_owner + 1
    scales = coded_ref[pl.ds(per_owner, devices, stride=pitch), :]

    def halves(words):
        return ((words << 16) >> 16).astype(jnp.float32), (words >> 16).astype(jnp.float32)

    grains = [
        jnp.transpose(jnp.exp2(code * (1.0 / SCALE_STEPS)) * (1.0 / CODE_MAX))[:per_owner]
        for code in halves(scales)
    ]
    for owner in range(owners):
        totals = [0.0, 0.0]
        for slab in range(slabs):
            source = owner * slabs + slab
            values = halves(coded_ref[source * pitch : source * pitch + per_owner, :])
            for i in range(2):
                totals[i] = totals[i] + values[i] * grains[i][:, source : source + 1]
        for i in range(2):
            out_ref[i, owner] = totals[i].astype(out_ref.dtype)


def on_device(amps, symmetry, screen, owner, integrals):
    owners, slabs = lax.axis_size("pair"), lax.axis_size("slab")
    devices = owners * slabs
    local_rows, tiles, width = amps.shape
    per_owner = tiles // owners
    tiles_here = per_owner // slabs
    rows_here, columns = integrals.shape[1:]
    everyone = ("pair", "slab")
    owner = owner.reshape(-1, LANES)
    symmetry = symmetry.reshape(-1, LANES)
    in_vmem = pl.BlockSpec(memory_space=pltpu.VMEM)
    params = pltpu.CompilerParams(vmem_limit_bytes=VMEM_LIMIT)

    ordered = pl.pallas_call(
        functools.partial(order_kernel, owners),
        out_shape=jax.ShapeDtypeStruct((tiles, local_rows * width), amps.dtype),
        in_specs=[in_vmem, in_vmem],
        out_specs=in_vmem,
        compiler_params=params,
        name="order_amps",
    )(owner, amps)
    arrived = lax.all_to_all(
        ordered.reshape(devices, tiles_here, local_rows * width), everyone, 0, 0, tiled=True
    ).reshape(devices * tiles_here, local_rows * width)

    masked = pl.pallas_call(
        functools.partial(mask_kernel, owners),
        grid=(tiles_here,),
        out_shape=pltpu.VMEM((rows_here, columns), integrals.dtype),
        in_specs=[
            in_vmem,
            in_vmem,
            in_vmem,
            pl.BlockSpec((None, width, columns), lambda k: (0, k, 0)),
        ],
        out_specs=in_vmem,
        scratch_shapes=[pltpu.VMEM((per_owner, columns), jnp.float32)],
        compiler_params=params,
        cost_estimate=pl.CostEstimate(
            flops=rows_here * columns, bytes_accessed=4 * rows_here * columns, transcendentals=0
        ),
        name="mask_block",
    )(owner, symmetry, screen, integrals)

    pitch = per_owner + 1
    coded = pl.pallas_call(
        functools.partial(partial_kernel, devices, local_rows),
        out_shape=jax.ShapeDtypeStruct((devices * pitch, width), jnp.int32),
        in_specs=[in_vmem, in_vmem],
        out_specs=in_vmem,
        scratch_shapes=[
            pltpu.VMEM((local_rows, devices * tiles_here, width), jnp.float32),
            pltpu.VMEM((devices * local_rows, rows_here), amps.dtype),
        ],
        compiler_params=params,
        name="partial_sums",
    )(arrived, masked)
    returned = lax.all_to_all(
        coded.reshape(devices, 1, pitch * width), everyone, 0, 0, tiled=True
    ).reshape(devices * pitch, width)

    return pl.pallas_call(
        functools.partial(total_kernel, slabs),
        out_shape=jax.ShapeDtypeStruct((local_rows, owners, per_owner, width), amps.dtype),
        in_specs=[in_vmem],
        out_specs=in_vmem,
        compiler_params=params,
        name="total",
    )(returned)


def solution(mesh):
    in_specs = (
        P(("pair", "slab"), None, None),
        P(),
        P("pair", None, None),
        P(),
        P("pair", "slab", None),
    )
    out_specs = P(("pair", "slab"), None, None, None)
    return jax.shard_map(
        on_device, mesh=mesh, in_specs=in_specs, out_specs=out_specs, check_vma=False
    )
```

```python
import functools

import jax
import jax.numpy as jnp
from jax import lax
from jax.experimental import pallas as pl
from jax.experimental.pallas import tpu as pltpu
from jax.sharding import PartitionSpec as P

LANES = 128
CODE_MAX = 32767.0
SCALE_STEPS = 128.0
LEAST = 1e-37
RESIDENT = 3 << 20


def tile_places(owner_ref, owners, per_owner):
    pieces = owner_ref.shape[0]
    tiles = pieces * LANES
    rows = lax.broadcasted_iota(jnp.int32, (owners, LANES), 0)
    held = jnp.concatenate(
        [(owner_ref[j : j + 1, :] == rows).astype(jnp.float32) for j in range(pieces)], axis=1
    )
    earlier = (
        lax.broadcasted_iota(jnp.int32, (tiles, tiles), 0)
        < lax.broadcasted_iota(jnp.int32, (tiles, tiles), 1)
    ).astype(jnp.bfloat16)
    rank = jnp.dot(held.astype(jnp.bfloat16), earlier, preferred_element_type=jnp.float32)
    first = lax.broadcasted_iota(jnp.int32, (owners, tiles), 0).astype(jnp.float32) * per_owner
    return jnp.sum(held * (first + rank), axis=0, keepdims=True)


def fetch(source, target, sem):
    copy = pltpu.make_async_copy(source, target, sem)
    copy.start()
    return copy


def order_kernel(owners, owner_hbm, amps_hbm, out_ref, owner_ref, amps_ref, sems):
    local_rows, tiles, width = amps_ref.shape
    owner_copy = fetch(owner_hbm, owner_ref, sems.at[0])
    amps_copy = fetch(amps_hbm, amps_ref, sems.at[1])
    owner_copy.wait()
    place = tile_places(owner_ref, owners, tiles // owners)
    rows = lax.broadcasted_iota(jnp.int32, (tiles, tiles), 0).astype(jnp.float32)
    pick = (rows == place).astype(jnp.bfloat16)
    amps_copy.wait()
    for i in range(local_rows):
        out_ref[:, i * width : (i + 1) * width] = jnp.dot(
            pick, amps_ref[i], preferred_element_type=jnp.float32
        ).astype(out_ref.dtype)


def mask_kernel(
    owners,
    owner_hbm,
    symmetry_hbm,
    screen_hbm,
    block_hbm,
    allowed_ref,
    out_ref,
    owner_ref,
    symmetry_ref,
    screen_ref,
    sems,
    block_sems,
):
    per_owner, columns = allowed_ref.shape
    width = LANES
    tiles_here = out_ref.shape[0] // width
    kept = out_ref.shape[1]
    small = [
        fetch(owner_hbm, owner_ref, sems.at[0]),
        fetch(symmetry_hbm, symmetry_ref, sems.at[1]),
        fetch(screen_hbm, screen_ref, sems.at[2]),
    ]
    spans = [slice(k * width, (k + 1) * width) for k in range(tiles_here)]
    blocks = [
        fetch(block_hbm.at[0, rows, 0:kept], out_ref.at[rows, :], block_sems.at[k])
        for k, rows in enumerate(spans)
    ]
    for copy in small:
        copy.wait()
    pieces = owner_ref.shape[0]
    tiles = pieces * LANES
    place = tile_places(owner_ref, owners, per_owner)
    first = lax.axis_index("pair") * per_owner
    rows = (lax.broadcasted_iota(jnp.int32, (per_owner, tiles), 0) + first).astype(jnp.float32)
    mine = (rows == place).astype(jnp.bfloat16)
    classes = lax.broadcasted_iota(jnp.int32, (16, LANES), 0)
    kinds = jnp.concatenate(
        [(symmetry_ref[j : j + 1, :] == classes).astype(jnp.float32) for j in range(pieces)],
        axis=1,
    ).astype(jnp.bfloat16)
    across = (((1,), (1,)), ((), ()))
    labels = lax.dot_general(mine, kinds, across, preferred_element_type=jnp.float32)
    labels = labels.astype(jnp.bfloat16)
    same = lax.dot_general(labels, labels, across, preferred_element_type=jnp.float32)
    allowed = jnp.where(screen_ref[0] == 1, same, 0.0).astype(jnp.bfloat16)
    spread = (
        lax.broadcasted_iota(jnp.int32, (per_owner, columns), 1) // LANES
        == lax.broadcasted_iota(jnp.int32, (per_owner, columns), 0)
    ).astype(jnp.bfloat16)
    allowed_ref[...] = jnp.dot(allowed, spread, preferred_element_type=jnp.float32)
    first = lax.axis_index("slab") * tiles_here
    for k, rows in enumerate(spans):
        keep = allowed_ref[pl.ds(first + k, 1), 0:kept].astype(out_ref.dtype)
        blocks[k].wait()
        out_ref[rows, :] = out_ref[rows, :] * keep


def partial_kernel(
    devices,
    local_rows,
    amps_ref,
    allowed_ref,
    masked_ref,
    block_hbm,
    out_ref,
    flat,
    operand,
    rest_ref,
    sems,
):
    width = LANES
    rows_here, kept = masked_ref.shape
    tiles_here = rows_here // width
    columns = allowed_ref.shape[1]
    per_owner = columns // width
    pitch = per_owner + 1
    chunk = 2 * width
    late = {
        start: fetch(
            block_hbm.at[0, :, start : start + chunk],
            rest_ref.at[:, start - kept : start - kept + chunk],
            sems.at[n],
        )
        for n, start in enumerate(range(kept, columns, chunk))
    }
    for i in range(local_rows):
        flat[i] = amps_ref[:, i * width : (i + 1) * width].astype(jnp.float32)
        for k in range(tiles_here):
            operand[i * devices : (i + 1) * devices, k * width : (k + 1) * width] = flat[
                i, pl.ds(k, devices, stride=tiles_here), :
            ].astype(operand.dtype)
    first = lax.axis_index("slab") * tiles_here
    lane = lax.broadcasted_iota(jnp.int32, (devices, width), 1)
    scales = jnp.zeros((devices, width), jnp.int32)
    for pair in range(per_owner // 2):
        start = pair * chunk
        if start < kept:
            masked = masked_ref[:, start : start + chunk]
        else:
            keep = [
                allowed_ref[pl.ds(first + k, 1), start : start + chunk].astype(rest_ref.dtype)
                for k in range(tiles_here)
            ]
            late[start].wait()
            masked = jnp.concatenate(
                [
                    rest_ref[k * width : (k + 1) * width, start - kept : start - kept + chunk]
                    * keep[k]
                    for k in range(tiles_here)
                ],
                axis=0,
            )
        summed = jnp.dot(operand[...], masked, preferred_element_type=jnp.float32)
        for half in range(2):
            tile = pair * 2 + half
            words = []
            for i in range(2):
                value = summed[i * devices : (i + 1) * devices, half * width : (half + 1) * width]
                top = jnp.maximum(jnp.max(jnp.abs(value), axis=1, keepdims=True), LEAST)
                code = jnp.ceil(jnp.log2(top) * SCALE_STEPS) + 1.0
                grain = jnp.exp2(code * (-1.0 / SCALE_STEPS)) * CODE_MAX
                words.append(
                    (jnp.floor(value * grain + 0.5).astype(jnp.int32), code.astype(jnp.int32))
                )
            (low, low_code), (high, high_code) = words
            out_ref[pl.ds(tile, devices, stride=pitch), :] = (high << 16) | (low & 0xFFFF)
            scales = jnp.where(lane == tile, (high_code << 16) | (low_code & 0xFFFF), scales)
    out_ref[pl.ds(per_owner, devices, stride=pitch), :] = scales


def total_kernel(slabs, coded_ref, out_ref):
    local_rows, owners, per_owner, width = out_ref.shape
    devices = owners * slabs
    pitch = per_owner + 1
    scales = coded_ref[pl.ds(per_owner, devices, stride=pitch), :]

    def halves(words):
        return ((words << 16) >> 16).astype(jnp.float32), (words >> 16).astype(jnp.float32)

    grains = [
        jnp.transpose(jnp.exp2(code * (1.0 / SCALE_STEPS)) * (1.0 / CODE_MAX))[:per_owner]
        for code in halves(scales)
    ]
    for owner in range(owners):
        totals = [0.0, 0.0]
        for slab in range(slabs):
            source = owner * slabs + slab
            values = halves(coded_ref[source * pitch : source * pitch + per_owner, :])
            for i in range(2):
                totals[i] = totals[i] + values[i] * grains[i][:, source : source + 1]
        for i in range(2):
            out_ref[i, owner] = totals[i].astype(out_ref.dtype)


def on_device(amps, symmetry, screen, owner, integrals):
    owners, slabs = lax.axis_size("pair"), lax.axis_size("slab")
    devices = owners * slabs
    local_rows, tiles, width = amps.shape
    per_owner = tiles // owners
    tiles_here = per_owner // slabs
    rows_here, columns = integrals.shape[1:]
    everyone = ("pair", "slab")
    owner = owner.reshape(-1, LANES)
    symmetry = symmetry.reshape(-1, LANES)
    in_vmem = pl.BlockSpec(memory_space=pltpu.VMEM)
    in_hbm = pl.BlockSpec(memory_space=pl.ANY)
    dma = pltpu.SemaphoreType.DMA
    alone = pltpu.CompilerParams(vmem_limit_bytes=60 << 20)
    beside = pltpu.CompilerParams(vmem_limit_bytes=48 << 20)
    small = pltpu.CompilerParams(vmem_limit_bytes=16 << 20)
    chunk = 2 * width
    kept = min(columns, RESIDENT // (rows_here * integrals.dtype.itemsize) // chunk * chunk)
    rest = max(columns - kept, chunk)

    ordered = pl.pallas_call(
        functools.partial(order_kernel, owners),
        out_shape=jax.ShapeDtypeStruct((tiles, local_rows * width), amps.dtype),
        in_specs=[in_hbm, in_hbm],
        out_specs=in_vmem,
        scratch_shapes=[
            pltpu.VMEM(owner.shape, owner.dtype),
            pltpu.VMEM(amps.shape, amps.dtype),
            dma((2,)),
        ],
        compiler_params=alone,
        name="order_amps",
    )(owner, amps)
    arrived = lax.all_to_all(
        ordered.reshape(devices, tiles_here, local_rows * width), everyone, 0, 0, tiled=True
    ).reshape(devices * tiles_here, local_rows * width)

    allowed, masked = pl.pallas_call(
        functools.partial(mask_kernel, owners),
        out_shape=(
            pltpu.VMEM((per_owner, columns), jnp.float32),
            pltpu.VMEM((rows_here, kept), integrals.dtype),
        ),
        in_specs=[in_hbm] * 4,
        out_specs=(in_vmem, in_vmem),
        scratch_shapes=[
            pltpu.VMEM(owner.shape, owner.dtype),
            pltpu.VMEM(symmetry.shape, symmetry.dtype),
            pltpu.VMEM(screen.shape, screen.dtype),
            dma((3,)),
            dma((tiles_here,)),
        ],
        compiler_params=beside,
        cost_estimate=pl.CostEstimate(
            flops=rows_here * columns, bytes_accessed=4 * rows_here * columns, transcendentals=0
        ),
        name="mask_block",
    )(owner, symmetry, screen, integrals)

    pitch = per_owner + 1
    coded = pl.pallas_call(
        functools.partial(partial_kernel, devices, local_rows),
        out_shape=jax.ShapeDtypeStruct((devices * pitch, width), jnp.int32),
        in_specs=[in_vmem, in_vmem, in_vmem, in_hbm],
        out_specs=in_vmem,
        scratch_shapes=[
            pltpu.VMEM((local_rows, devices * tiles_here, width), jnp.float32),
            pltpu.VMEM((devices * local_rows, rows_here), amps.dtype),
            pltpu.VMEM((rows_here, rest), integrals.dtype),
            dma((rest // chunk,)),
        ],
        compiler_params=beside,
        name="partial_sums",
    )(arrived, allowed, masked, integrals)
    returned = lax.all_to_all(
        coded.reshape(devices, 1, pitch * width), everyone, 0, 0, tiled=True
    ).reshape(devices * pitch, width)

    return pl.pallas_call(
        functools.partial(total_kernel, slabs),
        out_shape=jax.ShapeDtypeStruct((local_rows, owners, per_owner, width), amps.dtype),
        in_specs=[in_vmem],
        out_specs=in_vmem,
        compiler_params=small,
        name="total",
    )(returned)


def solution(mesh):
    in_specs = (
        P(("pair", "slab"), None, None),
        P(),
        P("pair", None, None),
        P(),
        P("pair", "slab", None),
    )
    out_specs = P(("pair", "slab"), None, None, None)
    return jax.shard_map(
        on_device, mesh=mesh, in_specs=in_specs, out_specs=out_specs, check_vma=False
    )
```

```python
import functools

import jax
import jax.numpy as jnp
from jax import lax
from jax.experimental import pallas as pl
from jax.experimental.pallas import tpu as pltpu
from jax.sharding import PartitionSpec as P

LANES = 128
CODE_MAX = 32767.0
SCALE_STEPS = 128.0
LEAST = 1e-37
RESIDENT = 13 << 18


def tile_places(owner_ref, owners, per_owner):
    pieces = owner_ref.shape[0]
    tiles = pieces * LANES
    rows = lax.broadcasted_iota(jnp.int32, (owners, LANES), 0)
    held = jnp.concatenate(
        [(owner_ref[j : j + 1, :] == rows).astype(jnp.float32) for j in range(pieces)], axis=1
    )
    earlier = (
        lax.broadcasted_iota(jnp.int32, (tiles, tiles), 0)
        < lax.broadcasted_iota(jnp.int32, (tiles, tiles), 1)
    ).astype(jnp.bfloat16)
    rank = jnp.dot(held.astype(jnp.bfloat16), earlier, preferred_element_type=jnp.float32)
    first = lax.broadcasted_iota(jnp.int32, (owners, tiles), 0).astype(jnp.float32) * per_owner
    return jnp.sum(held * (first + rank), axis=0, keepdims=True)


def fetch(source, target, sem):
    copy = pltpu.make_async_copy(source, target, sem)
    copy.start()
    return copy


def order_kernel(owners, owner_hbm, amps_hbm, out_ref, owner_ref, amps_ref, sems):
    local_rows, tiles, width = amps_ref.shape
    owner_copy = fetch(owner_hbm, owner_ref, sems.at[0])
    amps_copy = fetch(amps_hbm, amps_ref, sems.at[1])
    owner_copy.wait()
    place = tile_places(owner_ref, owners, tiles // owners)
    rows = lax.broadcasted_iota(jnp.int32, (tiles, tiles), 0).astype(jnp.float32)
    pick = (rows == place).astype(jnp.bfloat16)
    amps_copy.wait()
    for i in range(local_rows):
        out_ref[:, i * width : (i + 1) * width] = jnp.dot(
            pick, amps_ref[i], preferred_element_type=jnp.float32
        ).astype(out_ref.dtype)


def mask_kernel(
    owners,
    owner_hbm,
    symmetry_hbm,
    screen_hbm,
    block_hbm,
    rest_ref,
    out_ref,
    owner_ref,
    symmetry_ref,
    screen_ref,
    wide,
    sems,
    block_sems,
):
    per_owner, columns = wide.shape
    width = LANES
    tiles_here = out_ref.shape[0] // width
    kept = out_ref.shape[1]
    small = [
        fetch(owner_hbm, owner_ref, sems.at[0]),
        fetch(symmetry_hbm, symmetry_ref, sems.at[1]),
        fetch(screen_hbm, screen_ref, sems.at[2]),
    ]
    spans = [slice(k * width, (k + 1) * width) for k in range(tiles_here)]
    blocks = [
        fetch(block_hbm.at[0, rows, 0:kept], out_ref.at[rows, :], block_sems.at[k])
        for k, rows in enumerate(spans)
    ]
    for copy in small:
        copy.wait()
    pieces = owner_ref.shape[0]
    tiles = pieces * LANES
    place = tile_places(owner_ref, owners, per_owner)
    first = lax.axis_index("pair") * per_owner
    rows = (lax.broadcasted_iota(jnp.int32, (per_owner, tiles), 0) + first).astype(jnp.float32)
    mine = (rows == place).astype(jnp.bfloat16)
    classes = lax.broadcasted_iota(jnp.int32, (16, LANES), 0)
    kinds = jnp.concatenate(
        [(symmetry_ref[j : j + 1, :] == classes).astype(jnp.float32) for j in range(pieces)],
        axis=1,
    ).astype(jnp.bfloat16)
    across = (((1,), (1,)), ((), ()))
    labels = lax.dot_general(mine, kinds, across, preferred_element_type=jnp.float32)
    labels = labels.astype(jnp.bfloat16)
    same = lax.dot_general(labels, labels, across, preferred_element_type=jnp.float32)
    allowed = jnp.where(screen_ref[0] == 1, same, 0.0).astype(jnp.bfloat16)
    spread = (
        lax.broadcasted_iota(jnp.int32, (per_owner, columns), 1) // LANES
        == lax.broadcasted_iota(jnp.int32, (per_owner, columns), 0)
    ).astype(jnp.bfloat16)
    wide[...] = jnp.dot(allowed, spread, preferred_element_type=jnp.float32)
    first = lax.axis_index("slab") * tiles_here
    for k in range(tiles_here):
        rest_ref[k : k + 1, :] = wide[pl.ds(first + k, 1), columns - rest_ref.shape[1] :]
    for k, rows in enumerate(spans):
        keep = wide[pl.ds(first + k, 1), 0:kept].astype(out_ref.dtype)
        blocks[k].wait()
        out_ref[rows, :] = out_ref[rows, :] * keep


def partial_kernel(
    devices,
    local_rows,
    amps_ref,
    allowed_ref,
    masked_ref,
    block_hbm,
    out_ref,
    flat,
    operand,
    rest_ref,
    sums,
    sem,
):
    width = LANES
    rows_here, kept = masked_ref.shape
    tiles_here = rows_here // width
    columns = block_hbm.shape[2]
    per_owner = columns // width
    pitch = per_owner + 1
    late = fetch(block_hbm.at[0, :, kept:columns], rest_ref, sem) if kept < columns else None
    for i in range(local_rows):
        flat[i] = amps_ref[:, i * width : (i + 1) * width].astype(jnp.float32)
        for k in range(tiles_here):
            operand[i * devices : (i + 1) * devices, k * width : (k + 1) * width] = flat[
                i, pl.ds(k, devices, stride=tiles_here), :
            ].astype(operand.dtype)

    def column_tile(tile):
        start = tile * width
        if start < kept:
            return masked_ref[:, start : start + width]
        return jnp.concatenate(
            [
                rest_ref[k * width : (k + 1) * width, start - kept : start - kept + width]
                * allowed_ref[k : k + 1, start - kept : start - kept + width].astype(rest_ref.dtype)
                for k in range(tiles_here)
            ],
            axis=0,
        )

    top = jnp.full((local_rows * devices, width), LEAST, jnp.float32)
    for pair in range(per_owner // 2):
        start = pair * 2 * width
        if start + 2 * width <= kept:
            columns_here = masked_ref[:, start : start + 2 * width]
        else:
            if late is not None:
                late.wait()
                late = None
            columns_here = jnp.concatenate([column_tile(pair * 2), column_tile(pair * 2 + 1)], axis=1)
        summed = jnp.dot(operand[...], columns_here, preferred_element_type=jnp.float32)
        sums[:, start : start + 2 * width] = summed
        for half in range(2):
            top = jnp.maximum(top, jnp.abs(summed[:, half * width : (half + 1) * width]))
    code = jnp.ceil(jnp.log2(top) * SCALE_STEPS) + 1.0
    grain = jnp.exp2(code * (-1.0 / SCALE_STEPS)) * CODE_MAX

    def pack(words):
        return (words[devices:] << 16) | (words[:devices] & 0xFFFF)

    out_ref[pl.ds(per_owner, devices, stride=pitch), :] = pack(code.astype(jnp.int32))
    for tile in range(per_owner):
        value = sums[:, tile * width : (tile + 1) * width]
        out_ref[pl.ds(tile, devices, stride=pitch), :] = pack(
            jnp.floor(value * grain + 0.5).astype(jnp.int32)
        )


def total_kernel(slabs, coded_ref, out_hbm, out_ref, sems):
    local_rows, owners, per_owner, width = out_ref.shape
    devices = owners * slabs
    pitch = per_owner + 1
    scales = coded_ref[pl.ds(per_owner, devices, stride=pitch), :]

    def halves(words):
        return ((words << 16) >> 16).astype(jnp.float32), (words >> 16).astype(jnp.float32)

    grains = [
        jnp.exp2(code * (1.0 / SCALE_STEPS)) * (1.0 / CODE_MAX) for code in halves(scales)
    ]
    copies = []
    group = owners // sems.shape[0]
    for owner in range(owners):
        totals = [0.0, 0.0]
        for slab in range(slabs):
            source = owner * slabs + slab
            values = halves(coded_ref[source * pitch : source * pitch + per_owner, :])
            for i in range(2):
                totals[i] = totals[i] + values[i] * grains[i][source : source + 1, :]
        for i in range(2):
            out_ref[i, owner] = totals[i].astype(out_ref.dtype)
        if (owner + 1) % group == 0:
            done = slice(owner + 1 - group, owner + 1)
            copies.append(fetch(out_ref.at[:, done], out_hbm.at[:, done], sems.at[owner // group]))
    for copy in copies:
        copy.wait()


def on_device(amps, symmetry, screen, owner, integrals):
    owners, slabs = lax.axis_size("pair"), lax.axis_size("slab")
    devices = owners * slabs
    local_rows, tiles, width = amps.shape
    per_owner = tiles // owners
    tiles_here = per_owner // slabs
    rows_here, columns = integrals.shape[1:]
    everyone = ("pair", "slab")
    owner = owner.reshape(-1, LANES)
    symmetry = symmetry.reshape(-1, LANES)
    in_vmem = pl.BlockSpec(memory_space=pltpu.VMEM)
    in_hbm = pl.BlockSpec(memory_space=pl.ANY)
    dma = pltpu.SemaphoreType.DMA
    alone = pltpu.CompilerParams(vmem_limit_bytes=60 << 20)
    beside = pltpu.CompilerParams(vmem_limit_bytes=48 << 20)
    small = pltpu.CompilerParams(vmem_limit_bytes=16 << 20)
    kept = min(columns, RESIDENT // (rows_here * integrals.dtype.itemsize) // width * width)
    rest = max(columns - kept, 2 * width)

    ordered = pl.pallas_call(
        functools.partial(order_kernel, owners),
        out_shape=jax.ShapeDtypeStruct((tiles, local_rows * width), amps.dtype),
        in_specs=[in_hbm, in_hbm],
        out_specs=in_vmem,
        scratch_shapes=[
            pltpu.VMEM(owner.shape, owner.dtype),
            pltpu.VMEM(amps.shape, amps.dtype),
            dma((2,)),
        ],
        compiler_params=alone,
        name="order_amps",
    )(owner, amps)
    arrived = lax.all_to_all(
        ordered.reshape(devices, tiles_here, local_rows * width), everyone, 0, 0, tiled=True
    ).reshape(devices * tiles_here, local_rows * width)

    allowed, masked = pl.pallas_call(
        functools.partial(mask_kernel, owners),
        out_shape=(
            pltpu.VMEM((tiles_here, rest), jnp.float32),
            pltpu.VMEM((rows_here, kept), integrals.dtype),
        ),
        in_specs=[in_hbm] * 4,
        out_specs=(in_vmem, in_vmem),
        scratch_shapes=[
            pltpu.VMEM(owner.shape, owner.dtype),
            pltpu.VMEM(symmetry.shape, symmetry.dtype),
            pltpu.VMEM(screen.shape, screen.dtype),
            pltpu.VMEM((per_owner, columns), jnp.float32),
            dma((3,)),
            dma((tiles_here,)),
        ],
        compiler_params=beside,
        cost_estimate=pl.CostEstimate(
            flops=rows_here * columns, bytes_accessed=4 * rows_here * columns, transcendentals=0
        ),
        name="mask_block",
    )(owner, symmetry, screen, integrals)

    pitch = per_owner + 1
    coded = pl.pallas_call(
        functools.partial(partial_kernel, devices, local_rows),
        out_shape=jax.ShapeDtypeStruct((devices * pitch, width), jnp.int32),
        in_specs=[in_vmem, in_vmem, in_vmem, in_hbm],
        out_specs=in_vmem,
        scratch_shapes=[
            pltpu.VMEM((local_rows, devices * tiles_here, width), jnp.float32),
            pltpu.VMEM((devices * local_rows, rows_here), amps.dtype),
            pltpu.VMEM((rows_here, rest), integrals.dtype),
            pltpu.VMEM((devices * local_rows, columns), jnp.float32),
            dma,
        ],
        compiler_params=beside,
        name="partial_sums",
    )(arrived, allowed, masked, integrals)
    returned = lax.all_to_all(
        coded.reshape(devices, 1, pitch * width), everyone, 0, 0, tiled=True
    ).reshape(devices * pitch, width)

    return pl.pallas_call(
        functools.partial(total_kernel, slabs),
        out_shape=jax.ShapeDtypeStruct((local_rows, owners, per_owner, width), amps.dtype),
        in_specs=[in_vmem],
        out_specs=in_hbm,
        scratch_shapes=[
            pltpu.VMEM((local_rows, owners, per_owner, width), amps.dtype),
            dma((4,)),
        ],
        compiler_params=small,
        name="total",
    )(returned)


def solution(mesh):
    in_specs = (
        P(("pair", "slab"), None, None),
        P(),
        P("pair", None, None),
        P(),
        P("pair", "slab", None),
    )
    out_specs = P(("pair", "slab"), None, None, None)
    return jax.shard_map(
        on_device, mesh=mesh, in_specs=in_specs, out_specs=out_specs, check_vma=False
    )
```

```python
import functools

import jax
import jax.numpy as jnp
from jax import lax
from jax.experimental import pallas as pl
from jax.experimental.pallas import tpu as pltpu
from jax.sharding import PartitionSpec as P

LANES = 128
CODE_MAX = 32767.0
SCALE_STEPS = 128.0
LEAST = 1e-37
RESIDENT = 13 << 18


def earlier_tiles(tiles):
    return (
        lax.broadcasted_iota(jnp.int32, (tiles, tiles), 0)
        < lax.broadcasted_iota(jnp.int32, (tiles, tiles), 1)
    ).astype(jnp.bfloat16)


def tile_ranks(owner_ref, owners, earlier):
    rows = lax.broadcasted_iota(jnp.int32, (owners, LANES), 0)
    held = jnp.concatenate(
        [(owner_ref[j : j + 1, :] == rows).astype(jnp.float32) for j in range(owner_ref.shape[0])],
        axis=1,
    )
    return held, jnp.dot(held.astype(jnp.bfloat16), earlier, preferred_element_type=jnp.float32)


def fetch(source, target, sem):
    copy = pltpu.make_async_copy(source, target, sem)
    copy.start()
    return copy


def order_kernel(owners, slabs, owner_hbm, amps_hbm, out_ref, owner_ref, amps_ref, sems):
    local_rows, tiles, width = amps_ref.shape
    tiles_here = tiles // (owners * slabs)
    owner_copy = fetch(owner_hbm, owner_ref, sems.at[0])
    amps_copy = fetch(amps_hbm, amps_ref, sems.at[1])
    earlier = earlier_tiles(tiles)
    rows = lax.broadcasted_iota(jnp.int32, (tiles, tiles), 0).astype(jnp.float32)
    first = lax.broadcasted_iota(jnp.int32, (owners, tiles), 0).astype(jnp.float32) * tiles_here
    owner_copy.wait()
    held, rank = tile_ranks(owner_ref, owners, earlier)
    slab = jnp.floor((rank + 0.5) * (1.0 / tiles_here))
    place = first + rank + slab * ((owners - 1) * tiles_here)
    pick = (rows == jnp.sum(held * place, axis=0, keepdims=True)).astype(jnp.bfloat16)
    amps_copy.wait()
    for i in range(local_rows):
        out_ref[:, i * width : (i + 1) * width] = jnp.dot(
            pick, amps_ref[i], preferred_element_type=jnp.float32
        ).astype(out_ref.dtype)


def mask_kernel(
    owners,
    owner_hbm,
    symmetry_hbm,
    screen_hbm,
    block_hbm,
    rest_ref,
    out_ref,
    owner_ref,
    symmetry_ref,
    screen_ref,
    wide,
    sems,
    block_sems,
):
    per_owner, columns = wide.shape
    width = LANES
    tiles_here = out_ref.shape[0] // width
    kept = out_ref.shape[1]
    small = [
        fetch(owner_hbm, owner_ref, sems.at[0]),
        fetch(symmetry_hbm, symmetry_ref, sems.at[1]),
        fetch(screen_hbm, screen_ref, sems.at[2]),
    ]
    spans = [slice(k * width, (k + 1) * width) for k in range(tiles_here)]
    blocks = [
        fetch(block_hbm.at[0, rows, 0:kept], out_ref.at[rows, :], block_sems.at[k])
        for k, rows in enumerate(spans)
    ]
    pieces = owner_ref.shape[0]
    tiles = pieces * LANES
    earlier = earlier_tiles(tiles)
    for copy in small:
        copy.wait()
    held, rank = tile_ranks(owner_ref, owners, earlier)
    here = lax.broadcasted_iota(jnp.int32, (owners, tiles), 0) == lax.axis_index("pair")
    rank = jnp.sum(jnp.where(here, held * (rank + 1.0), 0.0), axis=0, keepdims=True) - 1.0
    rows = lax.broadcasted_iota(jnp.int32, (per_owner, tiles), 0).astype(jnp.float32)
    mine = (rows == rank).astype(jnp.bfloat16)
    classes = lax.broadcasted_iota(jnp.int32, (16, LANES), 0)
    kinds = jnp.concatenate(
        [(symmetry_ref[j : j + 1, :] == classes).astype(jnp.float32) for j in range(pieces)],
        axis=1,
    ).astype(jnp.bfloat16)
    across = (((1,), (1,)), ((), ()))
    labels = lax.dot_general(mine, kinds, across, preferred_element_type=jnp.float32)
    labels = labels.astype(jnp.bfloat16)
    same = lax.dot_general(labels, labels, across, preferred_element_type=jnp.float32)
    allowed = jnp.where(screen_ref[0] == 1, same, 0.0).astype(jnp.bfloat16)
    spread = (
        lax.broadcasted_iota(jnp.int32, (per_owner, columns), 1) // LANES
        == lax.broadcasted_iota(jnp.int32, (per_owner, columns), 0)
    ).astype(jnp.bfloat16)
    wide[...] = jnp.dot(allowed, spread, preferred_element_type=jnp.float32)
    first = lax.axis_index("slab") * tiles_here
    for k in range(tiles_here):
        rest_ref[k : k + 1, :] = wide[pl.ds(first + k, 1), columns - rest_ref.shape[1] :]
    for k, rows in enumerate(spans):
        keep = wide[pl.ds(first + k, 1), 0:kept].astype(out_ref.dtype)
        blocks[k].wait()
        out_ref[rows, :] = out_ref[rows, :] * keep


def partial_kernel(
    devices,
    local_rows,
    amps_ref,
    allowed_ref,
    masked_ref,
    block_hbm,
    out_ref,
    flat,
    operand,
    rest_ref,
    sums,
    sem,
):
    width = LANES
    rows_here, kept = masked_ref.shape
    tiles_here = rows_here // width
    columns = block_hbm.shape[2]
    per_owner = columns // width
    pitch = per_owner + 1
    late = fetch(block_hbm.at[0, :, kept:columns], rest_ref, sem) if kept < columns else None
    for i in range(local_rows):
        flat[i] = amps_ref[:, i * width : (i + 1) * width].astype(jnp.float32)
        for k in range(tiles_here):
            operand[i * devices : (i + 1) * devices, k * width : (k + 1) * width] = flat[
                i, pl.ds(k, devices, stride=tiles_here), :
            ].astype(operand.dtype)

    def column_tile(tile):
        start = tile * width
        if start < kept:
            return masked_ref[:, start : start + width]
        return jnp.concatenate(
            [
                rest_ref[k * width : (k + 1) * width, start - kept : start - kept + width]
                * allowed_ref[k : k + 1, start - kept : start - kept + width].astype(rest_ref.dtype)
                for k in range(tiles_here)
            ],
            axis=0,
        )

    top = jnp.full((local_rows * devices, width), LEAST, jnp.float32)
    for pair in range(per_owner // 2):
        start = pair * 2 * width
        if start + 2 * width <= kept:
            columns_here = masked_ref[:, start : start + 2 * width]
        else:
            if late is not None:
                late.wait()
                late = None
            columns_here = jnp.concatenate([column_tile(pair * 2), column_tile(pair * 2 + 1)], axis=1)
        summed = jnp.dot(operand[...], columns_here, preferred_element_type=jnp.float32)
        sums[:, start : start + 2 * width] = summed
        for half in range(2):
            top = jnp.maximum(top, jnp.abs(summed[:, half * width : (half + 1) * width]))
    code = jnp.ceil(jnp.log2(top) * SCALE_STEPS) + 1.0
    grain = jnp.exp2(code * (-1.0 / SCALE_STEPS)) * CODE_MAX

    def pack(words):
        return (words[devices:] << 16) | (words[:devices] & 0xFFFF)

    out_ref[pl.ds(per_owner, devices, stride=pitch), :] = pack(code.astype(jnp.int32))
    for tile in range(per_owner):
        value = sums[:, tile * width : (tile + 1) * width]
        out_ref[pl.ds(tile, devices, stride=pitch), :] = pack(
            jnp.floor(value * grain + 0.5).astype(jnp.int32)
        )


def total_kernel(slabs, coded_ref, out_hbm, out_ref, sems):
    local_rows, owners, per_owner, width = out_ref.shape
    devices = owners * slabs
    pitch = per_owner + 1
    scales = coded_ref[pl.ds(per_owner, devices, stride=pitch), :]

    def halves(words):
        return ((words << 16) >> 16).astype(jnp.float32), (words >> 16).astype(jnp.float32)

    grains = [
        jnp.exp2(code * (1.0 / SCALE_STEPS)) * (1.0 / CODE_MAX) for code in halves(scales)
    ]
    copies = []
    group = owners // sems.shape[0]
    for owner in range(owners):
        totals = [0.0, 0.0]
        for slab in range(slabs):
            source = slab * owners + owner
            values = halves(coded_ref[source * pitch : source * pitch + per_owner, :])
            for i in range(2):
                totals[i] = totals[i] + values[i] * grains[i][source : source + 1, :]
        for i in range(2):
            out_ref[i, owner] = totals[i].astype(out_ref.dtype)
        if (owner + 1) % group == 0:
            done = slice(owner + 1 - group, owner + 1)
            copies.append(fetch(out_ref.at[:, done], out_hbm.at[:, done], sems.at[owner // group]))
    for copy in copies:
        copy.wait()


def pinned(array):
    return pltpu.with_memory_space_constraint(array, pltpu.HBM)


def on_device(amps, symmetry, screen, owner, integrals):
    owners, slabs = lax.axis_size("pair"), lax.axis_size("slab")
    devices = owners * slabs
    local_rows, tiles, width = amps.shape
    per_owner = tiles // owners
    tiles_here = per_owner // slabs
    rows_here, columns = integrals.shape[1:]
    everyone = ("slab", "pair")
    owner = owner.reshape(-1, LANES)
    symmetry = symmetry.reshape(-1, LANES)
    in_vmem = pl.BlockSpec(memory_space=pltpu.VMEM)
    in_hbm = pl.BlockSpec(memory_space=pltpu.HBM)
    dma = pltpu.SemaphoreType.DMA
    beside = pltpu.CompilerParams(vmem_limit_bytes=48 << 20)
    small = pltpu.CompilerParams(vmem_limit_bytes=16 << 20)
    kept = min(columns, RESIDENT // (rows_here * integrals.dtype.itemsize) // width * width)
    rest = max(columns - kept, 2 * width)

    ordered = pl.pallas_call(
        functools.partial(order_kernel, owners, slabs),
        out_shape=jax.ShapeDtypeStruct((tiles, local_rows * width), amps.dtype),
        in_specs=[in_hbm, in_hbm],
        out_specs=in_vmem,
        scratch_shapes=[
            pltpu.VMEM(owner.shape, owner.dtype),
            pltpu.VMEM(amps.shape, amps.dtype),
            dma((2,)),
        ],
        compiler_params=beside,
        name="order_amps",
    )(pinned(owner), pinned(amps))
    arrived = lax.all_to_all(
        ordered.reshape(devices, tiles_here, local_rows * width), everyone, 0, 0, tiled=True
    ).reshape(devices * tiles_here, local_rows * width)

    allowed, masked = pl.pallas_call(
        functools.partial(mask_kernel, owners),
        out_shape=(
            pltpu.VMEM((tiles_here, rest), jnp.float32),
            pltpu.VMEM((rows_here, kept), integrals.dtype),
        ),
        in_specs=[in_hbm] * 4,
        out_specs=(in_vmem, in_vmem),
        scratch_shapes=[
            pltpu.VMEM(owner.shape, owner.dtype),
            pltpu.VMEM(symmetry.shape, symmetry.dtype),
            pltpu.VMEM(screen.shape, screen.dtype),
            pltpu.VMEM((per_owner, columns), jnp.float32),
            dma((3,)),
            dma((tiles_here,)),
        ],
        compiler_params=beside,
        cost_estimate=pl.CostEstimate(
            flops=rows_here * columns, bytes_accessed=4 * rows_here * columns, transcendentals=0
        ),
        name="mask_block",
    )(pinned(owner), pinned(symmetry), pinned(screen), pinned(integrals))

    pitch = per_owner + 1
    coded = pl.pallas_call(
        functools.partial(partial_kernel, devices, local_rows),
        out_shape=jax.ShapeDtypeStruct((devices * pitch, width), jnp.int32),
        in_specs=[in_vmem, in_vmem, in_vmem, in_hbm],
        out_specs=in_vmem,
        scratch_shapes=[
            pltpu.VMEM((local_rows, devices * tiles_here, width), jnp.float32),
            pltpu.VMEM((devices * local_rows, rows_here), amps.dtype),
            pltpu.VMEM((rows_here, rest), integrals.dtype),
            pltpu.VMEM((devices * local_rows, columns), jnp.float32),
            dma,
        ],
        compiler_params=beside,
        name="partial_sums",
    )(arrived, allowed, masked, pinned(integrals))
    returned = lax.all_to_all(
        coded.reshape(devices, 1, pitch * width), everyone, 0, 0, tiled=True
    ).reshape(devices * pitch, width)

    return pl.pallas_call(
        functools.partial(total_kernel, slabs),
        out_shape=jax.ShapeDtypeStruct((local_rows, owners, per_owner, width), amps.dtype),
        in_specs=[in_vmem],
        out_specs=in_hbm,
        scratch_shapes=[
            pltpu.VMEM((local_rows, owners, per_owner, width), amps.dtype),
            dma((4,)),
        ],
        compiler_params=small,
        name="total",
    )(returned)


def solution(mesh):
    in_specs = (
        P(("pair", "slab"), None, None),
        P(),
        P("pair", None, None),
        P(),
        P("pair", "slab", None),
    )
    out_specs = P(("pair", "slab"), None, None, None)
    return jax.shard_map(
        on_device, mesh=mesh, in_specs=in_specs, out_specs=out_specs, check_vma=False
    )
```

```python
import functools

import jax
import jax.numpy as jnp
import numpy as np
from jax import lax
from jax.experimental import pallas as pl
from jax.experimental.pallas import tpu as pltpu
from jax.sharding import PartitionSpec as P

LANES = 128
CODE_MAX = 32767.0
BIAS = 32768.0
SCALE_STEPS = 128.0
LEAST = 1e-33
ORDER_SEED = 22
RESIDENT = 13 << 18


def exchange_order(devices):
    order = np.random.RandomState(ORDER_SEED).permutation(devices)
    return [int(device) for device in order], [int(place) for place in np.argsort(order)]


def earlier_tiles(tiles):
    return (
        lax.broadcasted_iota(jnp.int32, (tiles, tiles), 0)
        < lax.broadcasted_iota(jnp.int32, (tiles, tiles), 1)
    ).astype(jnp.bfloat16)


def tile_ranks(owner_ref, owners, earlier):
    rows = lax.broadcasted_iota(jnp.int32, (owners, LANES), 0)
    held = jnp.concatenate(
        [(owner_ref[j : j + 1, :] == rows).astype(jnp.float32) for j in range(owner_ref.shape[0])],
        axis=1,
    )
    return held, jnp.dot(held.astype(jnp.bfloat16), earlier, preferred_element_type=jnp.float32)


def fetch(source, target, sem):
    copy = pltpu.make_async_copy(source, target, sem)
    copy.start()
    return copy


def order_kernel(owners, slabs, places, owner_hbm, amps_hbm, out_ref, owner_ref, amps_ref, sems):
    local_rows, tiles, width = amps_hbm.shape
    tiles_here = tiles // (owners * slabs)
    owner_copy = fetch(owner_hbm, owner_ref, sems.at[0])
    amps_copies = [
        fetch(amps_hbm.at[i], amps_ref.at[:, i * width : (i + 1) * width], sems.at[1 + i])
        for i in range(local_rows)
    ]
    earlier = earlier_tiles(tiles)
    rows = lax.broadcasted_iota(jnp.int32, (tiles, tiles), 0).astype(jnp.float32)
    holder = lax.broadcasted_iota(jnp.int32, (owners, LANES), 0)
    bases = []
    for index in range(slabs):
        base = jnp.zeros((owners, LANES), jnp.float32)
        for device in range(owners):
            entry = (places[index * owners + device] - index) * tiles_here
            base = jnp.where(holder == device, float(entry), base)
        bases.append(jnp.concatenate([base] * (tiles // LANES), axis=1))
    owner_copy.wait()
    held, rank = tile_ranks(owner_ref, owners, earlier)
    slab = jnp.floor((rank + 0.5) * (1.0 / tiles_here))
    place = rank
    for index, base in enumerate(bases):
        place = place + jnp.where(slab == index, base, 0.0)
    pick = (rows == jnp.sum(held * place, axis=0, keepdims=True)).astype(jnp.bfloat16)
    for copy in amps_copies:
        copy.wait()
    out_ref[...] = jnp.dot(pick, amps_ref[...], preferred_element_type=jnp.float32).astype(
        out_ref.dtype
    )


def mask_kernel(
    owners,
    owner_hbm,
    symmetry_hbm,
    screen_hbm,
    block_hbm,
    rest_ref,
    out_ref,
    owner_ref,
    symmetry_ref,
    screen_ref,
    wide,
    sems,
    block_sems,
):
    per_owner, columns = wide.shape
    width = LANES
    tiles_here = out_ref.shape[0] // width
    kept = out_ref.shape[1]
    small = [
        fetch(owner_hbm, owner_ref, sems.at[0]),
        fetch(symmetry_hbm, symmetry_ref, sems.at[1]),
        fetch(screen_hbm, screen_ref, sems.at[2]),
    ]
    spans = [slice(k * width, (k + 1) * width) for k in range(tiles_here)]
    blocks = [
        fetch(block_hbm.at[0, rows, 0:kept], out_ref.at[rows, :], block_sems.at[k])
        for k, rows in enumerate(spans)
    ]
    pieces = owner_ref.shape[0]
    tiles = pieces * LANES
    earlier = earlier_tiles(tiles)
    for copy in small:
        copy.wait()
    held, rank = tile_ranks(owner_ref, owners, earlier)
    here = lax.broadcasted_iota(jnp.int32, (owners, tiles), 0) == lax.axis_index("pair")
    rank = jnp.sum(jnp.where(here, held * (rank + 1.0), 0.0), axis=0, keepdims=True) - 1.0
    rows = lax.broadcasted_iota(jnp.int32, (per_owner, tiles), 0).astype(jnp.float32)
    mine = (rows == rank).astype(jnp.bfloat16)
    classes = lax.broadcasted_iota(jnp.int32, (16, LANES), 0)
    kinds = jnp.concatenate(
        [(symmetry_ref[j : j + 1, :] == classes).astype(jnp.float32) for j in range(pieces)],
        axis=1,
    ).astype(jnp.bfloat16)
    across = (((1,), (1,)), ((), ()))
    labels = lax.dot_general(mine, kinds, across, preferred_element_type=jnp.float32)
    labels = labels.astype(jnp.bfloat16)
    same = lax.dot_general(labels, labels, across, preferred_element_type=jnp.float32)
    allowed = jnp.where(screen_ref[0] == 1, same, 0.0).astype(jnp.bfloat16)
    spread = (
        lax.broadcasted_iota(jnp.int32, (per_owner, columns), 1) // LANES
        == lax.broadcasted_iota(jnp.int32, (per_owner, columns), 0)
    ).astype(jnp.bfloat16)
    wide[...] = jnp.dot(allowed, spread, preferred_element_type=jnp.float32)
    first = lax.axis_index("slab") * tiles_here
    for k in range(tiles_here):
        rest_ref[k : k + 1, :] = wide[pl.ds(first + k, 1), columns - rest_ref.shape[1] :]
    for k, rows in enumerate(spans):
        keep = wide[pl.ds(first + k, 1), 0:kept].astype(out_ref.dtype)
        blocks[k].wait()
        out_ref[rows, :] = out_ref[rows, :] * keep


def partial_kernel(
    devices,
    local_rows,
    amps_ref,
    allowed_ref,
    masked_ref,
    block_hbm,
    out_ref,
    flat,
    operand,
    rest_ref,
    sums,
    sem,
):
    width = LANES
    rows_here, kept = masked_ref.shape
    tiles_here = rows_here // width
    columns = block_hbm.shape[2]
    per_owner = columns // width
    pitch = per_owner + 1
    late = fetch(block_hbm.at[0, :, kept:columns], rest_ref, sem) if kept < columns else None
    for i in range(local_rows):
        flat[i] = amps_ref[:, i * width : (i + 1) * width].astype(jnp.float32)
        for k in range(tiles_here):
            operand[i * devices : (i + 1) * devices, k * width : (k + 1) * width] = flat[
                i, pl.ds(k, devices, stride=tiles_here), :
            ].astype(operand.dtype)

    def column_tile(tile):
        start = tile * width
        if start < kept:
            return masked_ref[:, start : start + width]
        return jnp.concatenate(
            [
                rest_ref[k * width : (k + 1) * width, start - kept : start - kept + width]
                * allowed_ref[k : k + 1, start - kept : start - kept + width].astype(rest_ref.dtype)
                for k in range(tiles_here)
            ],
            axis=0,
        )

    top = jnp.full((local_rows * devices, width), LEAST, jnp.float32)
    for pair in range(per_owner // 2):
        start = pair * 2 * width
        if start + 2 * width <= kept:
            columns_here = masked_ref[:, start : start + 2 * width]
        else:
            if late is not None:
                late.wait()
                late = None
            columns_here = jnp.concatenate([column_tile(pair * 2), column_tile(pair * 2 + 1)], axis=1)
        summed = jnp.dot(operand[...], columns_here, preferred_element_type=jnp.float32)
        sums[:, start : start + 2 * width] = summed
        for half in range(2):
            top = jnp.maximum(top, jnp.abs(summed[:, half * width : (half + 1) * width]))
    code = jnp.ceil(jnp.log2(top) * SCALE_STEPS) + 1.0
    grain = jnp.exp2(code * (-1.0 / SCALE_STEPS)) * CODE_MAX

    def pack(value):
        words = (value + (BIAS + 0.5)).astype(jnp.int32)
        return (words[devices:] << 16) | words[:devices]

    out_ref[pl.ds(per_owner, devices, stride=pitch), :] = pack(code)
    for tile in range(per_owner):
        value = sums[:, tile * width : (tile + 1) * width]
        out_ref[pl.ds(tile, devices, stride=pitch), :] = pack(value * grain)


def total_kernel(slabs, places, coded_ref, out_hbm, out_ref, sems):
    local_rows, owners, per_owner, width = out_ref.shape
    devices = owners * slabs
    pitch = per_owner + 1
    scales = coded_ref[pl.ds(per_owner, devices, stride=pitch), :]

    def halves(words):
        low, high = words & 0xFFFF, lax.shift_right_logical(words, 16)
        return low.astype(jnp.float32) - BIAS, high.astype(jnp.float32) - BIAS

    grains = [
        jnp.exp2(code * (1.0 / SCALE_STEPS)) * (1.0 / CODE_MAX) for code in halves(scales)
    ]
    copies = []
    group = owners // sems.shape[0]
    for owner in range(owners):
        totals = [0.0, 0.0]
        for slab in range(slabs):
            source = places[slab * owners + owner]
            values = halves(coded_ref[source * pitch : source * pitch + per_owner, :])
            for i in range(2):
                totals[i] = totals[i] + values[i] * grains[i][source : source + 1, :]
        for i in range(2):
            out_ref[i, owner] = totals[i].astype(out_ref.dtype)
        if (owner + 1) % group == 0:
            done = slice(owner + 1 - group, owner + 1)
            copies.append(fetch(out_ref.at[:, done], out_hbm.at[:, done], sems.at[owner // group]))
    for copy in copies:
        copy.wait()


def pinned(array):
    return pltpu.with_memory_space_constraint(array, pltpu.HBM)


def on_device(amps, symmetry, screen, owner, integrals):
    owners, slabs = lax.axis_size("pair"), lax.axis_size("slab")
    devices = owners * slabs
    local_rows, tiles, width = amps.shape
    per_owner = tiles // owners
    tiles_here = per_owner // slabs
    rows_here, columns = integrals.shape[1:]
    everyone = ("slab", "pair")
    order, places = exchange_order(devices)
    owner = owner.reshape(-1, LANES)
    symmetry = symmetry.reshape(-1, LANES)
    in_vmem = pl.BlockSpec(memory_space=pltpu.VMEM)
    in_hbm = pl.BlockSpec(memory_space=pltpu.HBM)
    dma = pltpu.SemaphoreType.DMA
    beside = pltpu.CompilerParams(vmem_limit_bytes=48 << 20)
    small = pltpu.CompilerParams(vmem_limit_bytes=16 << 20)
    kept = min(columns, RESIDENT // (rows_here * integrals.dtype.itemsize) // width * width)
    rest = max(columns - kept, 2 * width)

    ordered = pl.pallas_call(
        functools.partial(order_kernel, owners, slabs, places),
        out_shape=jax.ShapeDtypeStruct((tiles, local_rows * width), amps.dtype),
        in_specs=[in_hbm] * 2,
        out_specs=in_vmem,
        scratch_shapes=[
            pltpu.VMEM(owner.shape, owner.dtype),
            pltpu.VMEM((tiles, local_rows * width), amps.dtype),
            dma((1 + local_rows,)),
        ],
        compiler_params=beside,
        name="order_amps",
    )(pinned(owner), pinned(amps))
    arrived = lax.all_to_all(
        ordered.reshape(devices, tiles_here, local_rows * width), everyone, 0, 0, tiled=True, axis_index_groups=[order]
    ).reshape(devices * tiles_here, local_rows * width)

    allowed, masked = pl.pallas_call(
        functools.partial(mask_kernel, owners),
        out_shape=(
            pltpu.VMEM((tiles_here, rest), jnp.float32),
            pltpu.VMEM((rows_here, kept), integrals.dtype),
        ),
        in_specs=[in_hbm] * 4,
        out_specs=(in_vmem, in_vmem),
        scratch_shapes=[
            pltpu.VMEM(owner.shape, owner.dtype),
            pltpu.VMEM(symmetry.shape, symmetry.dtype),
            pltpu.VMEM(screen.shape, screen.dtype),
            pltpu.VMEM((per_owner, columns), jnp.float32),
            dma((3,)),
            dma((tiles_here,)),
        ],
        compiler_params=beside,
        cost_estimate=pl.CostEstimate(
            flops=rows_here * columns, bytes_accessed=4 * rows_here * columns, transcendentals=0
        ),
        name="mask_block",
    )(pinned(owner), pinned(symmetry), pinned(screen), pinned(integrals))

    pitch = per_owner + 1
    coded = pl.pallas_call(
        functools.partial(partial_kernel, devices, local_rows),
        out_shape=jax.ShapeDtypeStruct((devices * pitch, width), jnp.int32),
        in_specs=[in_vmem, in_vmem, in_vmem, in_hbm],
        out_specs=in_vmem,
        scratch_shapes=[
            pltpu.VMEM((local_rows, devices * tiles_here, width), jnp.float32),
            pltpu.VMEM((devices * local_rows, rows_here), amps.dtype),
            pltpu.VMEM((rows_here, rest), integrals.dtype),
            pltpu.VMEM((devices * local_rows, columns), jnp.float32),
            dma,
        ],
        compiler_params=beside,
        name="partial_sums",
    )(arrived, allowed, masked, pinned(integrals))
    returned = lax.all_to_all(
        coded.reshape(devices, 1, pitch * width), everyone, 0, 0, tiled=True, axis_index_groups=[order]
    ).reshape(devices * pitch, width)

    return pl.pallas_call(
        functools.partial(total_kernel, slabs, places),
        out_shape=jax.ShapeDtypeStruct((local_rows, owners, per_owner, width), amps.dtype),
        in_specs=[in_vmem],
        out_specs=in_hbm,
        scratch_shapes=[
            pltpu.VMEM((local_rows, owners, per_owner, width), amps.dtype),
            dma((4,)),
        ],
        compiler_params=small,
        name="total",
    )(returned)


def solution(mesh):
    in_specs = (
        P(("pair", "slab"), None, None),
        P(),
        P("pair", None, None),
        P(),
        P("pair", "slab", None),
    )
    out_specs = P(("pair", "slab"), None, None, None)
    return jax.shard_map(
        on_device, mesh=mesh, in_specs=in_specs, out_specs=out_specs, check_vma=False
    )
```

```python
import functools

import jax
import jax.numpy as jnp
import numpy as np
from jax import lax
from jax.experimental import pallas as pl
from jax.experimental.pallas import tpu as pltpu
from jax.sharding import PartitionSpec as P

LANES = 128
CODE_MAX = 32767.0
BIAS = 32768.0
SCALE_STEPS = 128.0
LEAST = 1e-33
ORDER_SEED = 22
RESIDENT = 13 << 18


def exchange_order(devices):
    order = np.random.RandomState(ORDER_SEED).permutation(devices)
    return [int(device) for device in order], [int(place) for place in np.argsort(order)]


def earlier_tiles(tiles):
    return (
        lax.broadcasted_iota(jnp.int32, (tiles, tiles), 0)
        < lax.broadcasted_iota(jnp.int32, (tiles, tiles), 1)
    ).astype(jnp.bfloat16)


def tile_ranks(owner_ref, owners, earlier):
    rows = lax.broadcasted_iota(jnp.int32, (owners, LANES), 0)
    held = jnp.concatenate(
        [(owner_ref[j : j + 1, :] == rows).astype(jnp.float32) for j in range(owner_ref.shape[0])],
        axis=1,
    )
    return held, jnp.dot(held.astype(jnp.bfloat16), earlier, preferred_element_type=jnp.float32)


def fetch(source, target, sem):
    copy = pltpu.make_async_copy(source, target, sem)
    copy.start()
    return copy


def order_kernel(
    owners, slabs, places, owner_hbm, amps_hbm, out_hbm, owner_ref, amps_ref, out_ref, sems, out_sems
):
    local_rows, tiles, width = amps_hbm.shape
    tiles_here = tiles // (owners * slabs)
    owner_copy = fetch(owner_hbm, owner_ref, sems.at[0])
    amps_copies = [
        fetch(amps_hbm.at[i], amps_ref.at[:, i * width : (i + 1) * width], sems.at[1 + i])
        for i in range(local_rows)
    ]
    earlier = earlier_tiles(tiles)
    rows = lax.broadcasted_iota(jnp.int32, (tiles, tiles), 0).astype(jnp.float32)
    holder = lax.broadcasted_iota(jnp.int32, (owners, LANES), 0)
    bases = []
    for index in range(slabs):
        base = jnp.zeros((owners, LANES), jnp.float32)
        for device in range(owners):
            entry = (places[index * owners + device] - index) * tiles_here
            base = jnp.where(holder == device, float(entry), base)
        bases.append(jnp.concatenate([base] * (tiles // LANES), axis=1))
    owner_copy.wait()
    held, rank = tile_ranks(owner_ref, owners, earlier)
    slab = jnp.floor((rank + 0.5) * (1.0 / tiles_here))
    place = rank
    for index, base in enumerate(bases):
        place = place + jnp.where(slab == index, base, 0.0)
    pick = (rows == jnp.sum(held * place, axis=0, keepdims=True)).astype(jnp.bfloat16)
    for copy in amps_copies:
        copy.wait()
    copies = []
    for part in range(2):
        rows = slice(part * tiles // 2, (part + 1) * tiles // 2)
        out_ref[rows, :] = jnp.dot(
            pick[rows], amps_ref[...], preferred_element_type=jnp.float32
        ).astype(out_ref.dtype)
        copies.append(fetch(out_ref.at[rows, :], out_hbm.at[rows, :], out_sems.at[part]))
    for copy in copies:
        copy.wait()


def mask_kernel(
    owners,
    owner_hbm,
    symmetry_hbm,
    screen_hbm,
    block_hbm,
    rest_ref,
    out_ref,
    owner_ref,
    symmetry_ref,
    screen_ref,
    wide,
    sems,
    block_sems,
):
    per_owner, columns = wide.shape
    width = LANES
    tiles_here = out_ref.shape[0] // width
    kept = out_ref.shape[1]
    small = [
        fetch(owner_hbm, owner_ref, sems.at[0]),
        fetch(symmetry_hbm, symmetry_ref, sems.at[1]),
        fetch(screen_hbm, screen_ref, sems.at[2]),
    ]
    spans = [slice(k * width, (k + 1) * width) for k in range(tiles_here)]
    blocks = [
        fetch(block_hbm.at[0, rows, 0:kept], out_ref.at[rows, :], block_sems.at[k])
        for k, rows in enumerate(spans)
    ]
    pieces = owner_ref.shape[0]
    tiles = pieces * LANES
    earlier = earlier_tiles(tiles)
    for copy in small:
        copy.wait()
    held, rank = tile_ranks(owner_ref, owners, earlier)
    here = lax.broadcasted_iota(jnp.int32, (owners, tiles), 0) == lax.axis_index("pair")
    rank = jnp.sum(jnp.where(here, held * (rank + 1.0), 0.0), axis=0, keepdims=True) - 1.0
    rows = lax.broadcasted_iota(jnp.int32, (per_owner, tiles), 0).astype(jnp.float32)
    mine = (rows == rank).astype(jnp.bfloat16)
    classes = lax.broadcasted_iota(jnp.int32, (16, LANES), 0)
    kinds = jnp.concatenate(
        [(symmetry_ref[j : j + 1, :] == classes).astype(jnp.float32) for j in range(pieces)],
        axis=1,
    ).astype(jnp.bfloat16)
    across = (((1,), (1,)), ((), ()))
    labels = lax.dot_general(mine, kinds, across, preferred_element_type=jnp.float32)
    labels = labels.astype(jnp.bfloat16)
    same = lax.dot_general(labels, labels, across, preferred_element_type=jnp.float32)
    allowed = jnp.where(screen_ref[0] == 1, same, 0.0).astype(jnp.bfloat16)
    spread = (
        lax.broadcasted_iota(jnp.int32, (per_owner, columns), 1) // LANES
        == lax.broadcasted_iota(jnp.int32, (per_owner, columns), 0)
    ).astype(jnp.bfloat16)
    wide[...] = jnp.dot(allowed, spread, preferred_element_type=jnp.float32)
    first = lax.axis_index("slab") * tiles_here
    for k in range(tiles_here):
        rest_ref[k : k + 1, :] = wide[pl.ds(first + k, 1), columns - rest_ref.shape[1] :]
    for k, rows in enumerate(spans):
        keep = wide[pl.ds(first + k, 1), 0:kept].astype(out_ref.dtype)
        blocks[k].wait()
        out_ref[rows, :] = out_ref[rows, :] * keep


def partial_kernel(
    devices,
    local_rows,
    amps_ref,
    allowed_ref,
    masked_ref,
    block_hbm,
    out_ref,
    flat,
    operand,
    rest_ref,
    sums,
    sem,
):
    width = LANES
    rows_here, kept = masked_ref.shape
    tiles_here = rows_here // width
    columns = block_hbm.shape[2]
    per_owner = columns // width
    pitch = per_owner + 1
    late = fetch(block_hbm.at[0, :, kept:columns], rest_ref, sem) if kept < columns else None
    for i in range(local_rows):
        flat[i] = amps_ref[:, i * width : (i + 1) * width].astype(jnp.float32)
        for k in range(tiles_here):
            operand[i * devices : (i + 1) * devices, k * width : (k + 1) * width] = flat[
                i, pl.ds(k, devices, stride=tiles_here), :
            ].astype(operand.dtype)

    def column_tile(tile):
        start = tile * width
        if start < kept:
            return masked_ref[:, start : start + width]
        return jnp.concatenate(
            [
                rest_ref[k * width : (k + 1) * width, start - kept : start - kept + width]
                * allowed_ref[k : k + 1, start - kept : start - kept + width].astype(rest_ref.dtype)
                for k in range(tiles_here)
            ],
            axis=0,
        )

    top = jnp.full((local_rows * devices, width), LEAST, jnp.float32)
    for pair in range(per_owner // 2):
        start = pair * 2 * width
        if start + 2 * width <= kept:
            columns_here = masked_ref[:, start : start + 2 * width]
        else:
            if late is not None:
                late.wait()
                late = None
            columns_here = jnp.concatenate([column_tile(pair * 2), column_tile(pair * 2 + 1)], axis=1)
        summed = jnp.dot(operand[...], columns_here, preferred_element_type=jnp.float32)
        sums[:, start : start + 2 * width] = summed
        for half in range(2):
            top = jnp.maximum(top, jnp.abs(summed[:, half * width : (half + 1) * width]))
    code = jnp.ceil(jnp.log2(top) * SCALE_STEPS) + 1.0
    grain = jnp.exp2(code * (-1.0 / SCALE_STEPS)) * CODE_MAX

    def pack(value):
        words = (value + (BIAS + 0.5)).astype(jnp.int32)
        return (words[devices:] << 16) | words[:devices]

    out_ref[pl.ds(per_owner, devices, stride=pitch), :] = pack(code)
    for tile in range(per_owner):
        value = sums[:, tile * width : (tile + 1) * width]
        out_ref[pl.ds(tile, devices, stride=pitch), :] = pack(value * grain)


def total_kernel(slabs, places, coded_ref, out_hbm, out_ref, sems):
    local_rows, owners, per_owner, width = out_ref.shape
    devices = owners * slabs
    pitch = per_owner + 1
    scales = coded_ref[pl.ds(per_owner, devices, stride=pitch), :]

    def halves(words):
        low, high = words & 0xFFFF, lax.shift_right_logical(words, 16)
        return low.astype(jnp.float32) - BIAS, high.astype(jnp.float32) - BIAS

    grains = [
        jnp.exp2(code * (1.0 / SCALE_STEPS)) * (1.0 / CODE_MAX) for code in halves(scales)
    ]
    copies = []
    group = owners // sems.shape[0]
    for owner in range(owners):
        totals = [0.0, 0.0]
        for slab in range(slabs):
            source = places[slab * owners + owner]
            values = halves(coded_ref[source * pitch : source * pitch + per_owner, :])
            for i in range(2):
                totals[i] = totals[i] + values[i] * grains[i][source : source + 1, :]
        for i in range(2):
            out_ref[i, owner] = totals[i].astype(out_ref.dtype)
        if (owner + 1) % group == 0:
            done = slice(owner + 1 - group, owner + 1)
            copies.append(fetch(out_ref.at[:, done], out_hbm.at[:, done], sems.at[owner // group]))
    for copy in copies:
        copy.wait()


def pinned(array):
    return pltpu.with_memory_space_constraint(array, pltpu.HBM)


def on_device(amps, symmetry, screen, owner, integrals):
    owners, slabs = lax.axis_size("pair"), lax.axis_size("slab")
    devices = owners * slabs
    local_rows, tiles, width = amps.shape
    per_owner = tiles // owners
    tiles_here = per_owner // slabs
    rows_here, columns = integrals.shape[1:]
    everyone = ("slab", "pair")
    order, places = exchange_order(devices)
    owner = owner.reshape(-1, LANES)
    symmetry = symmetry.reshape(-1, LANES)
    in_vmem = pl.BlockSpec(memory_space=pltpu.VMEM)
    in_hbm = pl.BlockSpec(memory_space=pltpu.HBM)
    dma = pltpu.SemaphoreType.DMA
    beside = pltpu.CompilerParams(vmem_limit_bytes=48 << 20)
    small = pltpu.CompilerParams(vmem_limit_bytes=16 << 20)
    kept = min(columns, RESIDENT // (rows_here * integrals.dtype.itemsize) // width * width)
    rest = max(columns - kept, 2 * width)

    ordered = pl.pallas_call(
        functools.partial(order_kernel, owners, slabs, places),
        out_shape=jax.ShapeDtypeStruct((tiles, local_rows * width), amps.dtype),
        in_specs=[in_hbm] * 2,
        out_specs=in_hbm,
        scratch_shapes=[
            pltpu.VMEM(owner.shape, owner.dtype),
            pltpu.VMEM((tiles, local_rows * width), amps.dtype),
            pltpu.VMEM((tiles, local_rows * width), amps.dtype),
            dma((1 + local_rows,)),
            dma((2,)),
        ],
        compiler_params=beside,
        name="order_amps",
    )(pinned(owner), pinned(amps))
    arrived = lax.all_to_all(
        ordered.reshape(devices, tiles_here, local_rows * width), everyone, 0, 0, tiled=True, axis_index_groups=[order]
    ).reshape(devices * tiles_here, local_rows * width)

    allowed, masked = pl.pallas_call(
        functools.partial(mask_kernel, owners),
        out_shape=(
            pltpu.VMEM((tiles_here, rest), jnp.float32),
            pltpu.VMEM((rows_here, kept), integrals.dtype),
        ),
        in_specs=[in_hbm] * 4,
        out_specs=(in_vmem, in_vmem),
        scratch_shapes=[
            pltpu.VMEM(owner.shape, owner.dtype),
            pltpu.VMEM(symmetry.shape, symmetry.dtype),
            pltpu.VMEM(screen.shape, screen.dtype),
            pltpu.VMEM((per_owner, columns), jnp.float32),
            dma((3,)),
            dma((tiles_here,)),
        ],
        compiler_params=beside,
        cost_estimate=pl.CostEstimate(
            flops=rows_here * columns, bytes_accessed=4 * rows_here * columns, transcendentals=0
        ),
        name="mask_block",
    )(pinned(owner), pinned(symmetry), pinned(screen), pinned(integrals))

    pitch = per_owner + 1
    coded = pl.pallas_call(
        functools.partial(partial_kernel, devices, local_rows),
        out_shape=jax.ShapeDtypeStruct((devices * pitch, width), jnp.int32),
        in_specs=[in_vmem, in_vmem, in_vmem, in_hbm],
        out_specs=in_vmem,
        scratch_shapes=[
            pltpu.VMEM((local_rows, devices * tiles_here, width), jnp.float32),
            pltpu.VMEM((devices * local_rows, rows_here), amps.dtype),
            pltpu.VMEM((rows_here, rest), integrals.dtype),
            pltpu.VMEM((devices * local_rows, columns), jnp.float32),
            dma,
        ],
        compiler_params=beside,
        name="partial_sums",
    )(arrived, allowed, masked, pinned(integrals))
    returned = lax.all_to_all(
        coded.reshape(devices, 1, pitch * width), everyone, 0, 0, tiled=True, axis_index_groups=[order]
    ).reshape(devices * pitch, width)

    return pl.pallas_call(
        functools.partial(total_kernel, slabs, places),
        out_shape=jax.ShapeDtypeStruct((local_rows, owners, per_owner, width), amps.dtype),
        in_specs=[in_vmem],
        out_specs=in_hbm,
        scratch_shapes=[
            pltpu.VMEM((local_rows, owners, per_owner, width), amps.dtype),
            dma((4,)),
        ],
        compiler_params=small,
        name="total",
    )(returned)


def solution(mesh):
    in_specs = (
        P(("pair", "slab"), None, None),
        P(),
        P("pair", None, None),
        P(),
        P("pair", "slab", None),
    )
    out_specs = P(("pair", "slab"), None, None, None)
    return jax.shard_map(
        on_device, mesh=mesh, in_specs=in_specs, out_specs=out_specs, check_vma=False
    )
```

```python
import functools

import jax
import jax.numpy as jnp
import numpy as np
from jax import lax
from jax.experimental import pallas as pl
from jax.experimental.pallas import tpu as pltpu
from jax.sharding import PartitionSpec as P

LANES = 128
CODE_MAX = 32767.0
BIAS = 32768.0
SCALE_STEPS = 128.0
LEAST = 1e-33
ORDER_SEED = 106
RESIDENT = 13 << 18


def exchange_order(devices):
    order = np.random.RandomState(ORDER_SEED).permutation(devices)
    return [int(device) for device in order], [int(place) for place in np.argsort(order)]


def earlier_tiles(tiles):
    return (
        lax.broadcasted_iota(jnp.int32, (tiles, tiles), 0)
        < lax.broadcasted_iota(jnp.int32, (tiles, tiles), 1)
    ).astype(jnp.bfloat16)


def tile_ranks(owner_ref, owners, earlier):
    rows = lax.broadcasted_iota(jnp.int32, (owners, LANES), 0)
    held = jnp.concatenate(
        [(owner_ref[j : j + 1, :] == rows).astype(jnp.float32) for j in range(owner_ref.shape[0])],
        axis=1,
    )
    return held, jnp.dot(held.astype(jnp.bfloat16), earlier, preferred_element_type=jnp.float32)


def fetch(source, target, sem):
    copy = pltpu.make_async_copy(source, target, sem)
    copy.start()
    return copy


def order_kernel(owners, slabs, places, owner_hbm, amps_hbm, out_ref, owner_ref, amps_ref, sems):
    local_rows, tiles, width = amps_hbm.shape
    tiles_here = tiles // (owners * slabs)
    owner_copy = fetch(owner_hbm, owner_ref, sems.at[0])
    amps_copies = [
        fetch(amps_hbm.at[i], amps_ref.at[:, i * width : (i + 1) * width], sems.at[1 + i])
        for i in range(local_rows)
    ]
    earlier = earlier_tiles(tiles)
    rows = lax.broadcasted_iota(jnp.int32, (tiles, tiles), 0).astype(jnp.float32)
    holder = lax.broadcasted_iota(jnp.int32, (owners, LANES), 0)
    bases = []
    for index in range(slabs):
        base = jnp.zeros((owners, LANES), jnp.float32)
        for device in range(owners):
            entry = (places[index * owners + device] - index) * tiles_here
            base = jnp.where(holder == device, float(entry), base)
        bases.append(jnp.concatenate([base] * (tiles // LANES), axis=1))
    owner_copy.wait()
    held, rank = tile_ranks(owner_ref, owners, earlier)
    slab = jnp.floor((rank + 0.5) * (1.0 / tiles_here))
    place = rank
    for index, base in enumerate(bases):
        place = place + jnp.where(slab == index, base, 0.0)
    pick = (rows == jnp.sum(held * place, axis=0, keepdims=True)).astype(jnp.bfloat16)
    for copy in amps_copies:
        copy.wait()
    out_ref[...] = jnp.dot(pick, amps_ref[...], preferred_element_type=jnp.float32).astype(
        out_ref.dtype
    )


def mask_kernel(
    owners,
    owner_hbm,
    symmetry_hbm,
    screen_hbm,
    block_hbm,
    rest_ref,
    out_ref,
    owner_ref,
    symmetry_ref,
    screen_ref,
    wide,
    sems,
    block_sems,
):
    per_owner, columns = wide.shape
    width = LANES
    tiles_here = out_ref.shape[0] // width
    kept = out_ref.shape[1]
    small = [
        fetch(owner_hbm, owner_ref, sems.at[0]),
        fetch(symmetry_hbm, symmetry_ref, sems.at[1]),
        fetch(screen_hbm, screen_ref, sems.at[2]),
    ]
    spans = [slice(k * width, (k + 1) * width) for k in range(tiles_here)]
    blocks = [
        fetch(block_hbm.at[0, rows, 0:kept], out_ref.at[rows, :], block_sems.at[k])
        for k, rows in enumerate(spans)
    ]
    pieces = owner_ref.shape[0]
    tiles = pieces * LANES
    earlier = earlier_tiles(tiles)
    for copy in small:
        copy.wait()
    held, rank = tile_ranks(owner_ref, owners, earlier)
    here = lax.broadcasted_iota(jnp.int32, (owners, tiles), 0) == lax.axis_index("pair")
    rank = jnp.sum(jnp.where(here, held * (rank + 1.0), 0.0), axis=0, keepdims=True) - 1.0
    rows = lax.broadcasted_iota(jnp.int32, (per_owner, tiles), 0).astype(jnp.float32)
    mine = (rows == rank).astype(jnp.bfloat16)
    classes = lax.broadcasted_iota(jnp.int32, (16, LANES), 0)
    kinds = jnp.concatenate(
        [(symmetry_ref[j : j + 1, :] == classes).astype(jnp.float32) for j in range(pieces)],
        axis=1,
    ).astype(jnp.bfloat16)
    across = (((1,), (1,)), ((), ()))
    labels = lax.dot_general(mine, kinds, across, preferred_element_type=jnp.float32)
    labels = labels.astype(jnp.bfloat16)
    same = lax.dot_general(labels, labels, across, preferred_element_type=jnp.float32)
    allowed = jnp.where(screen_ref[0] == 1, same, 0.0).astype(jnp.bfloat16)
    spread = (
        lax.broadcasted_iota(jnp.int32, (per_owner, columns), 1) // LANES
        == lax.broadcasted_iota(jnp.int32, (per_owner, columns), 0)
    ).astype(jnp.bfloat16)
    wide[...] = jnp.dot(allowed, spread, preferred_element_type=jnp.float32)
    first = lax.axis_index("slab") * tiles_here
    for k in range(tiles_here):
        rest_ref[k : k + 1, :] = wide[pl.ds(first + k, 1), columns - rest_ref.shape[1] :]
    for k, rows in enumerate(spans):
        keep = wide[pl.ds(first + k, 1), 0:kept].astype(out_ref.dtype)
        blocks[k].wait()
        out_ref[rows, :] = out_ref[rows, :] * keep


def partial_kernel(
    devices,
    local_rows,
    amps_ref,
    allowed_ref,
    masked_ref,
    block_hbm,
    out_ref,
    flat,
    operand,
    rest_ref,
    sums,
    sem,
):
    width = LANES
    rows_here, kept = masked_ref.shape
    tiles_here = rows_here // width
    columns = block_hbm.shape[2]
    per_owner = columns // width
    pitch = per_owner + 1
    late = fetch(block_hbm.at[0, :, kept:columns], rest_ref, sem) if kept < columns else None
    for i in range(local_rows):
        flat[i] = amps_ref[:, i * width : (i + 1) * width].astype(jnp.float32)
        for k in range(tiles_here):
            operand[i * devices : (i + 1) * devices, k * width : (k + 1) * width] = flat[
                i, pl.ds(k, devices, stride=tiles_here), :
            ].astype(operand.dtype)

    def column_tile(tile):
        start = tile * width
        if start < kept:
            return masked_ref[:, start : start + width]
        return jnp.concatenate(
            [
                rest_ref[k * width : (k + 1) * width, start - kept : start - kept + width]
                * allowed_ref[k : k + 1, start - kept : start - kept + width].astype(rest_ref.dtype)
                for k in range(tiles_here)
            ],
            axis=0,
        )

    top = jnp.full((local_rows * devices, width), LEAST, jnp.float32)
    for pair in range(per_owner // 2):
        start = pair * 2 * width
        if start + 2 * width <= kept:
            columns_here = masked_ref[:, start : start + 2 * width]
        else:
            if late is not None:
                late.wait()
                late = None
            columns_here = jnp.concatenate([column_tile(pair * 2), column_tile(pair * 2 + 1)], axis=1)
        summed = jnp.dot(operand[...], columns_here, preferred_element_type=jnp.float32)
        sums[:, start : start + 2 * width] = summed
        for half in range(2):
            top = jnp.maximum(top, jnp.abs(summed[:, half * width : (half + 1) * width]))
    code = jnp.ceil(jnp.log2(top) * SCALE_STEPS) + 1.0
    grain = jnp.exp2(code * (-1.0 / SCALE_STEPS)) * CODE_MAX

    def pack(value):
        words = (value + (BIAS + 0.5)).astype(jnp.int32)
        return (words[devices:] << 16) | words[:devices]

    out_ref[pl.ds(per_owner, devices, stride=pitch), :] = pack(code)
    for tile in range(per_owner):
        value = sums[:, tile * width : (tile + 1) * width]
        out_ref[pl.ds(tile, devices, stride=pitch), :] = pack(value * grain)


def total_kernel(slabs, places, coded_ref, out_hbm, out_ref, sems):
    local_rows, owners, per_owner, width = out_ref.shape
    devices = owners * slabs
    pitch = per_owner + 1
    scales = coded_ref[pl.ds(per_owner, devices, stride=pitch), :]

    def halves(words):
        low, high = words & 0xFFFF, lax.shift_right_logical(words, 16)
        return low.astype(jnp.float32) - BIAS, high.astype(jnp.float32) - BIAS

    grains = [
        jnp.exp2(code * (1.0 / SCALE_STEPS)) * (1.0 / CODE_MAX) for code in halves(scales)
    ]
    copies = []
    group = owners // sems.shape[0]
    for owner in range(owners):
        totals = [0.0, 0.0]
        for slab in range(slabs):
            source = places[slab * owners + owner]
            values = halves(coded_ref[source * pitch : source * pitch + per_owner, :])
            for i in range(2):
                totals[i] = totals[i] + values[i] * grains[i][source : source + 1, :]
        for i in range(2):
            out_ref[i, owner] = totals[i].astype(out_ref.dtype)
        if (owner + 1) % group == 0:
            done = slice(owner + 1 - group, owner + 1)
            copies.append(fetch(out_ref.at[:, done], out_hbm.at[:, done], sems.at[owner // group]))
    for copy in copies:
        copy.wait()


def pinned(array):
    return pltpu.with_memory_space_constraint(array, pltpu.HBM)


def on_device(amps, symmetry, screen, owner, integrals):
    owners, slabs = lax.axis_size("pair"), lax.axis_size("slab")
    devices = owners * slabs
    local_rows, tiles, width = amps.shape
    per_owner = tiles // owners
    tiles_here = per_owner // slabs
    rows_here, columns = integrals.shape[1:]
    everyone = ("slab", "pair")
    order, places = exchange_order(devices)
    owner = owner.reshape(-1, LANES)
    symmetry = symmetry.reshape(-1, LANES)
    in_vmem = pl.BlockSpec(memory_space=pltpu.VMEM)
    in_hbm = pl.BlockSpec(memory_space=pltpu.HBM)
    dma = pltpu.SemaphoreType.DMA
    beside = pltpu.CompilerParams(vmem_limit_bytes=48 << 20)
    small = pltpu.CompilerParams(vmem_limit_bytes=16 << 20)
    kept = min(columns, RESIDENT // (rows_here * integrals.dtype.itemsize) // width * width)
    rest = max(columns - kept, 2 * width)

    ordered = pl.pallas_call(
        functools.partial(order_kernel, owners, slabs, places),
        out_shape=jax.ShapeDtypeStruct((tiles, local_rows * width), amps.dtype),
        in_specs=[in_hbm] * 2,
        out_specs=in_vmem,
        scratch_shapes=[
            pltpu.VMEM(owner.shape, owner.dtype),
            pltpu.VMEM((tiles, local_rows * width), amps.dtype),
            dma((1 + local_rows,)),
        ],
        compiler_params=beside,
        name="order_amps",
    )(pinned(owner), pinned(amps))
    arrived = lax.all_to_all(
        ordered.reshape(devices, tiles_here, local_rows * width), everyone, 0, 0, tiled=True, axis_index_groups=[order]
    ).reshape(devices * tiles_here, local_rows * width)

    allowed, masked = pl.pallas_call(
        functools.partial(mask_kernel, owners),
        out_shape=(
            pltpu.VMEM((tiles_here, rest), jnp.float32),
            pltpu.VMEM((rows_here, kept), integrals.dtype),
        ),
        in_specs=[in_hbm] * 4,
        out_specs=(in_vmem, in_vmem),
        scratch_shapes=[
            pltpu.VMEM(owner.shape, owner.dtype),
            pltpu.VMEM(symmetry.shape, symmetry.dtype),
            pltpu.VMEM(screen.shape, screen.dtype),
            pltpu.VMEM((per_owner, columns), jnp.float32),
            dma((3,)),
            dma((tiles_here,)),
        ],
        compiler_params=beside,
        cost_estimate=pl.CostEstimate(
            flops=rows_here * columns, bytes_accessed=4 * rows_here * columns, transcendentals=0
        ),
        name="mask_block",
    )(pinned(owner), pinned(symmetry), pinned(screen), pinned(integrals))

    pitch = per_owner + 1
    coded = pl.pallas_call(
        functools.partial(partial_kernel, devices, local_rows),
        out_shape=jax.ShapeDtypeStruct((devices * pitch, width), jnp.int32),
        in_specs=[in_vmem, in_vmem, in_vmem, in_hbm],
        out_specs=in_vmem,
        scratch_shapes=[
            pltpu.VMEM((local_rows, devices * tiles_here, width), jnp.float32),
            pltpu.VMEM((devices * local_rows, rows_here), amps.dtype),
            pltpu.VMEM((rows_here, rest), integrals.dtype),
            pltpu.VMEM((devices * local_rows, columns), jnp.float32),
            dma,
        ],
        compiler_params=beside,
        name="partial_sums",
    )(arrived, allowed, masked, pinned(integrals))
    returned = lax.all_to_all(
        coded.reshape(devices, 1, pitch * width), everyone, 0, 0, tiled=True, axis_index_groups=[order]
    ).reshape(devices * pitch, width)

    return pl.pallas_call(
        functools.partial(total_kernel, slabs, places),
        out_shape=jax.ShapeDtypeStruct((local_rows, owners, per_owner, width), amps.dtype),
        in_specs=[in_vmem],
        out_specs=in_hbm,
        scratch_shapes=[
            pltpu.VMEM((local_rows, owners, per_owner, width), amps.dtype),
            dma((4,)),
        ],
        compiler_params=small,
        name="total",
    )(returned)


def solution(mesh):
    in_specs = (
        P(("pair", "slab"), None, None),
        P(),
        P("pair", None, None),
        P(),
        P("pair", "slab", None),
    )
    out_specs = P(("pair", "slab"), None, None, None)
    return jax.shard_map(
        on_device, mesh=mesh, in_specs=in_specs, out_specs=out_specs, check_vma=False
    )
```
